128 devices in a mesh: row: 8 (over x, y_hi), col: 16 (over z, y_lo, core).
Axes of the slice: x: 4, y: 4 (y_hi: 2, y_lo: 2; y = y_hi * 2 + y_lo), z: 4, core: 2. Of those that a mesh axis runs over, the one named last changes fastest.
Arguments:
- click_counts: int32 [16384, 16384], P('row', 'col'), may hold values from 1 to 2047, as said below
- tile_pattern: int32 [64, 64], P('row', 'col'), may hold values from 0 to 1, as said below
- row_factors: bfloat16 [16384, 512], P(('row', 'col')), may hold values from 0.25 to 6, as said below
- column_factors: bfloat16 [16384, 512], P(('col', 'row')), may hold values from 0.25 to 6, as said below
Outputs:
- updated_rows: bfloat16 [16384, 512], P(('row', 'col'))
- updated_columns: bfloat16 [16384, 512], P(('col', 'row'))
The draws below stay inside these ranges and needn't reach their ends.
Inputs may be any that keep to these rules, and one draw needn't show every extreme that they name: `click_counts`: whole numbers of clicks. `tile_pattern`: 1 marks a stored tile of 256 x 256 entries; the share of stored tiles differs strongly between blocks of 2048 x 1024 entries. `row_factors`: every entry is positive. `column_factors`: every entry is positive.
All inputs are finite; a program needn't handle non-finite values.
Results may differ from the reference program's by a relative error of at most 0.0026.
Values may be sent and summed in bfloat16 or wider, within the bound.
No kernel may reach another device: no remote copies, remote signals or barrier semaphores. Data moves between devices by JAX's collectives and lax.ppermute only.
A program may use at most 128 MiB of HBM per device.

```python
import jax
import jax.numpy as jnp
from jax import lax

K = 512
TILE = 256
ROW_DEV = 2048
COL_DEV = 1024
M = 16384
N = 16384


def topic_labels(key):
    row_topic = jax.random.randint(jax.random.fold_in(key, 21), (M,), 0, 8)
    col_topic = jax.random.randint(jax.random.fold_in(key, 22), (N,), 0, 8)
    return (row_topic, col_topic)


def shape_factors(baseline, topic, rows, position_ratio, lift):
    position = jnp.arange(rows, dtype=jnp.float32)[:, None] / max(rows - 1, 1)
    topic_group = jnp.arange(K, dtype=jnp.int32) // (K // 8)
    emphasis = jnp.where(topic_group[None, :] == topic[:, None], lift, 1.0)
    return (baseline * jnp.exp(jnp.log(position_ratio) * position) * emphasis).astype(jnp.bfloat16)


def draw_click_counts(key, part):
    row_topic, col_topic = topic_labels(key)
    key = jax.random.fold_in(key, 4)
    first_key, second_key, third_key, fourth_key = jax.random.split(key, 4)
    powers = jax.random.randint(first_key, (8, 8), 0, 4)
    affinity = jnp.left_shift(jnp.ones_like(powers), powers)
    pairing = affinity[row_topic[:, None], col_topic[None, :]]
    row_level = jax.random.randint(second_key, (M,), 1, 17)
    col_level = jax.random.randint(third_key, (N,), 1, 9)
    jitter = jax.random.randint(fourth_key, (M, N), 1, 5)
    product_counts = pairing * row_level[:, None] * col_level[None, :] * jitter
    counts = jnp.clip(product_counts, 1, 2047)
    counts = counts.at[0, 0].set(2047)
    counts = counts.at[0, 1].set(1)
    return counts.astype(jnp.int32)


def draw_tile_pattern(key, part):
    key = jax.random.fold_in(key, 3)
    first_key, second_key, third_key = jax.random.split(key, 3)
    grid_rows = M // TILE
    grid_cols = N // TILE
    tiles_down = ROW_DEV // TILE
    tiles_across = COL_DEV // TILE
    row_levels = jax.random.randint(first_key, (grid_rows // tiles_down,), 1, 5)
    col_levels = jax.random.randint(second_key, (grid_cols // tiles_across,), 1, 5)
    level = jnp.repeat(row_levels, tiles_down)[:, None] * jnp.repeat(col_levels, tiles_across)[None, :]
    chances = jax.random.randint(third_key, (grid_rows, grid_cols), 0, 16)
    return (chances < level).astype(jnp.int32)


def draw_row_factors(key, part):
    row_topic, col_topic = topic_labels(key)
    key = jax.random.fold_in(key, 1)
    spread_draw = jax.random.uniform(key, (M, K), jnp.float32)
    baseline = jnp.exp(jnp.log(0.25) + jnp.log(2.0) * spread_draw)
    return shape_factors(baseline, row_topic, M, 3.0, 3.95)


def draw_column_factors(key, part):
    row_topic, col_topic = topic_labels(key)
    key = jax.random.fold_in(key, 2)
    spread_draw = jax.random.uniform(key, (N, K), jnp.float32)
    baseline = jnp.exp(jnp.log(0.25) + jnp.log(2.0) * spread_draw)
    return shape_factors(baseline, col_topic, N, 3.0, 3.95)


def setup_inputs(seed: int = 0) -> dict:
    key_list = jax.random.split(jax.random.key(seed), 5)
    return {
        "click_counts": draw_click_counts(jax.random.fold_in(key_list[4], 71), 0),
        "tile_pattern": draw_tile_pattern(jax.random.fold_in(key_list[4], 71), 0),
        "row_factors": draw_row_factors(jax.random.fold_in(key_list[4], 71), 0),
        "column_factors": draw_column_factors(jax.random.fold_in(key_list[4], 71), 0),
    }


def ratio_block(left_block, count_block, live_row, column_factors):
    predicted = lax.dot_general(left_block, column_factors, (((1,), (1,)), ((), ())), preferred_element_type=jnp.float32)
    values = count_block.astype(jnp.float32) / predicted
    return jnp.where(live_row[None, :] > 0, values, jnp.zeros_like(values)).astype(jnp.bfloat16)


def reference(click_counts, tile_pattern, row_factors, column_factors):
    blocks = M // TILE
    column_total = jnp.sum(column_factors.astype(jnp.float32), axis=0)
    live_columns = jnp.repeat(tile_pattern, TILE, axis=1)
    count_blocks = click_counts.reshape(blocks, TILE, N)

    def numerator(inputs):
        left_block, count_block, live_row = inputs
        ratios = ratio_block(left_block, count_block, live_row, column_factors)
        return jnp.dot(ratios, column_factors, preferred_element_type=jnp.float32)

    row_sums = lax.map(numerator, (row_factors.reshape(blocks, TILE, K), count_blocks, live_columns)).reshape(M, K)
    updated_rows = (row_factors.astype(jnp.float32) * row_sums / column_total[None, :]).astype(jnp.bfloat16)
    row_total = jnp.sum(updated_rows.astype(jnp.float32), axis=0)

    def add_columns(totals, inputs):
        left_block, count_block, live_row = inputs
        ratios = ratio_block(left_block, count_block, live_row, column_factors)
        term = lax.dot_general(ratios, left_block, (((0,), (0,)), ((), ())), preferred_element_type=jnp.float32)
        return totals + term, None

    column_sums, _ = lax.scan(add_columns, jnp.zeros((N, K), jnp.float32), (updated_rows.reshape(blocks, TILE, K), count_blocks, live_columns))
    updated_columns = (column_factors.astype(jnp.float32) * column_sums / row_total[None, :]).astype(jnp.bfloat16)
    return (updated_rows, updated_columns)
```

```python
import functools

import jax
import jax.numpy as jnp
from jax import lax
from jax.experimental import pallas as pl
from jax.experimental.pallas import tpu as pltpu
from jax.sharding import PartitionSpec as P

WIRE = jnp.float16
ROW_SCALE = 2.0**-6
COLUMN_SCALE = 2.0**-11
BLOCK = 128
TILE = 256
F32 = jnp.float32


def along_z(step):
    return [(j, (j // 4 + step) % 4 * 4 + j % 4) for j in range(16)]


def along_x(step):
    return [(i, (i // 2 + step) % 4 * 2 + i % 2) for i in range(8)]


SWAP_CORE = [(j, j ^ 1) for j in range(16)]
SWAP_PAIR = [(j, j ^ 2) for j in range(16)]
SWAP_FAR = [(i, i ^ 1) for i in range(8)]


def contract_last(a, b):
    return lax.dot_general(a, b, (((1,), (1,)), ((), ())), preferred_element_type=F32)


def tile_ratios(counts, predicted, live_ref, row_tile, tiles_across):
    parts = []
    for j in range(tiles_across):
        window = slice(j * TILE, (j + 1) * TILE)
        live = live_ref[row_tile * tiles_across + j] > 0
        value = counts[:, window].astype(F32) / predicted[:, window]
        parts.append(jnp.where(live, value, 0.0).astype(jnp.bfloat16))
    return parts


def place_panel(place_ref, panel_ref, placed):
    for k in range(placed.shape[0]):
        placed[place_ref[k]] = panel_ref[k]


def rows_kernel(tiles_across, rows_ref, live_ref, place_ref, c0, c1, a, b, panel, keep, send, placed):
    step = pl.program_id(0)

    @pl.when(step == 0)
    def _():
        place_panel(place_ref, panel, placed)

    columns = placed[...].reshape(-1, placed.shape[-1])
    left = jnp.concatenate([a[0], b[0]], axis=0)
    counts = jnp.concatenate([c0[...], c1[...]], axis=0)
    predicted = contract_last(left, columns)
    ratios = tile_ratios(counts, predicted, live_ref, rows_ref[2 * step] // 2, tiles_across)
    total = jnp.dot(jnp.concatenate(ratios, axis=1), columns, preferred_element_type=F32)
    keep[0] = total[:BLOCK]
    send[0] = total[BLOCK:]


def columns_kernel(
    tiles_across, rows_ref, live_ref, place_ref, c0, c1, a, b, panel, keep, send, placed, total
):
    step = pl.program_id(0)

    @pl.when(step == 0)
    def _():
        place_panel(place_ref, panel, placed)
        total[...] = jnp.zeros_like(total)

    columns = placed[...].reshape(-1, placed.shape[-1])
    left = jnp.concatenate([a[0], b[0]], axis=0)
    counts = jnp.concatenate([c0[...], c1[...]], axis=0)
    predicted = contract_last(left, columns)
    ratios = tile_ratios(counts, predicted, live_ref, rows_ref[2 * step] // 2, tiles_across)
    for j in range(tiles_across):
        term = lax.dot_general(
            ratios[j], left, (((0,), (0,)), ((), ())), preferred_element_type=F32
        )
        total[2 * j] += term[:BLOCK]
        total[2 * j + 1] += term[BLOCK:]

    @pl.when(step == pl.num_programs(0) - 1)
    def _():
        for k in range(2):
            keep[k] = total[place_ref[k]]
        for k in range(2, 8):
            send[k - 2] = total[place_ref[k]]


def sweep(kernel, rows_at, live, columns_at, counts, own, other, panel, out_shape, out_specs, scratch):
    width = own.shape[-1]
    across = counts.shape[1]

    def counts_spec(half):
        return pl.BlockSpec((BLOCK, across), lambda g, rows, live, place: (rows[2 * g + half], 0))

    block = pl.BlockSpec((1, BLOCK, width), lambda g, rows, live, place: (g, 0, 0))
    grid_spec = pltpu.PrefetchScalarGridSpec(
        num_scalar_prefetch=3,
        grid=(8,),
        in_specs=[
            counts_spec(0),
            counts_spec(1),
            block,
            block,
            pl.BlockSpec(panel.shape, lambda g, rows, live, place: (0, 0, 0)),
        ],
        out_specs=out_specs,
        scratch_shapes=[pltpu.VMEM(panel.shape, panel.dtype)] + scratch,
    )
    flops = 4 * counts.shape[0] * across * width
    return pl.pallas_call(
        functools.partial(kernel, across // TILE),
        grid_spec=grid_spec,
        out_shape=out_shape,
        cost_estimate=pl.CostEstimate(
            flops=flops, bytes_accessed=4 * counts.size + 8 * own.size, transcendentals=0
        ),
        compiler_params=pltpu.CompilerParams(vmem_limit_bytes=48 * 2**20),
    )(rows_at, live, columns_at, counts, counts, own, other, panel)


def gather_z(pair):
    up = lax.ppermute(pair, "col", along_z(-1))
    down = lax.ppermute(pair, "col", along_z(1))
    far_up = lax.ppermute(up[0], "col", along_z(-1))
    far_down = lax.ppermute(down[1], "col", along_z(1))
    return jnp.concatenate([pair, up, far_up[None], far_down[None], down], axis=0)


def gather_x(pair):
    up = lax.ppermute(pair, "row", along_x(-1))
    down = lax.ppermute(pair, "row", along_x(1))
    far_up = lax.ppermute(up[0], "row", along_x(-1))
    far_down = lax.ppermute(down[1], "row", along_x(1))
    return jnp.concatenate([pair, up, far_up[None], far_down[None], down], axis=0)


def total_over_col(partial):
    partial = partial + lax.ppermute(partial, "col", SWAP_CORE)
    partial = partial + lax.ppermute(partial, "col", SWAP_PAIR)
    partial = partial + lax.ppermute(partial, "col", along_z(2))
    return partial + lax.ppermute(partial, "col", along_z(1))


def total_over_row(partial):
    partial = partial + lax.ppermute(partial, "row", SWAP_FAR)
    partial = partial + lax.ppermute(partial, "row", along_x(2))
    return partial + lax.ppermute(partial, "row", along_x(1))


def local(click_counts, tile_pattern, row_factors, column_factors):
    width = row_factors.shape[1]
    at_row, at_col = lax.axis_index("row"), lax.axis_index("col")
    z, pair, core = at_col // 4, at_col // 2 % 2, at_col % 2
    x, far = at_row // 2, at_row % 2
    rows_at = jnp.stack(
        [
            (z + dz) % 4 * 4 + (pair + dl) % 2 * 2 + (core + dc) % 2
            for dz in range(4)
            for dl in range(2)
            for dc in range(2)
        ]
    ).astype(jnp.int32)
    columns_at = jnp.stack(
        [(x + dx) % 4 * 2 + (far + dh) % 2 for dx in range(4) for dh in range(2)]
    ).astype(jnp.int32)
    live = tile_pattern.reshape(-1)

    with jax.named_scope("gather_in"):
        row_pair = jnp.stack([row_factors, lax.ppermute(row_factors, "col", SWAP_PAIR)])
        column_pair = jnp.stack([column_factors, lax.ppermute(column_factors, "row", SWAP_FAR)])
        own = gather_z(row_pair)
        panel = gather_x(column_pair)
        other = lax.ppermute(own, "col", SWAP_CORE)
    with jax.named_scope("column_total"):
        column_total = total_over_col(jnp.sum(panel.astype(F32), axis=(0, 1)))

    block = pl.BlockSpec((1, BLOCK, width), lambda g, rows, live, place: (g, 0, 0))
    keep, send = sweep(
        rows_kernel,
        rows_at,
        live,
        columns_at,
        click_counts,
        own,
        other,
        panel,
        (
            jax.ShapeDtypeStruct((8, BLOCK, width), F32),
            jax.ShapeDtypeStruct((8, BLOCK, width), F32),
        ),
        (block, block),
        [],
    )
    with jax.named_scope("reduce_rows"):
        came = lax.ppermute(send, "col", SWAP_CORE)
        partial = (keep + came) * ROW_SCALE
        packed = partial.astype(WIRE)
        arrived = [
            lax.ppermute(packed[2 * dz : 2 * dz + 2], "col", along_z(dz)) for dz in (1, 2, 3)
        ]
        partial = partial[:2] + sum(a.astype(F32) for a in arrived)
        packed = partial.astype(WIRE)
        came = lax.ppermute(packed, "col", SWAP_PAIR)
        share = (packed.astype(F32) + came[::-1].astype(F32)) * (1 / ROW_SCALE)
    updated_pair = (row_pair.astype(F32) * share / column_total).astype(jnp.bfloat16)
    with jax.named_scope("gather_new"):
        own = gather_z(updated_pair)
        other = lax.ppermute(own, "col", SWAP_CORE)
    with jax.named_scope("row_total"):
        row_total = total_over_row(
            jnp.sum(own.astype(F32), axis=(0, 1)) + jnp.sum(other.astype(F32), axis=(0, 1))
        )
    keep, send = sweep(
        columns_kernel,
        rows_at,
        live,
        columns_at,
        click_counts,
        own,
        other,
        panel,
        (
            jax.ShapeDtypeStruct((2, BLOCK, width), F32),
            jax.ShapeDtypeStruct((6, BLOCK, width), F32),
        ),
        (
            pl.BlockSpec((2, BLOCK, width), lambda g, rows, live, place: (0, 0, 0)),
            pl.BlockSpec((6, BLOCK, width), lambda g, rows, live, place: (0, 0, 0)),
        ),
        [pltpu.VMEM((8, BLOCK, width), F32)],
    )
    with jax.named_scope("reduce_columns"):
        send = (send * COLUMN_SCALE).astype(WIRE)
        arrived = [
            lax.ppermute(send[2 * dx - 2 : 2 * dx], "row", along_x(dx)) for dx in (1, 2, 3)
        ]
        partial = keep * COLUMN_SCALE + sum(a.astype(F32) for a in arrived)
        came = lax.ppermute(partial[1].astype(WIRE), "row", SWAP_FAR)
        share = (partial[0] + came.astype(F32)) * (1 / COLUMN_SCALE)
    updated_columns = (column_factors.astype(F32) * share / row_total).astype(jnp.bfloat16)
    return (updated_pair[0], updated_columns)


def solution(mesh):
    in_specs = (P("row", "col"), P("row", "col"), P(("row", "col"), None), P(("col", "row"), None))
    out_specs = (P(("row", "col"), None), P(("col", "row"), None))
    return jax.shard_map(local, mesh=mesh, in_specs=in_specs, out_specs=out_specs, check_vma=False)
```

```python
import functools

import jax
import jax.numpy as jnp
from jax import lax
from jax.experimental import pallas as pl
from jax.experimental.pallas import tpu as pltpu
from jax.sharding import PartitionSpec as P

WIRE = jnp.float16
ROW_SCALE = 2.0**-6
COLUMN_SCALE = 2.0**-9
COARSE_SCALE = 2.0**-5
FINE_SCALE = 2.0**14
FINE_LIMIT = 61440.0
BLOCK = 128
TILE = 256
F32 = jnp.float32


CHIP_GROUPS = [list(range(core, 16, 2)) for core in range(2)]
SWAP_CORE = [(j, j ^ 1) for j in range(16)]
PAD = 8


def contract_last(a, b):
    return lax.dot_general(a, b, (((1,), (1,)), ((), ())), preferred_element_type=F32)


def tile_ratios(counts, predicted, live_ref, row_tile, tiles_across):
    parts = []
    for j in range(tiles_across):
        window = slice(j * TILE, (j + 1) * TILE)
        live = live_ref[row_tile * tiles_across + j] > 0
        value = counts[:, window].astype(F32) / predicted[:, window]
        parts.append(jnp.where(live, value, 0.0).astype(jnp.bfloat16))
    return parts


def rows_kernel(tiles_across, rows_ref, live_ref, c0, c1, a, b, panel, keep, send):
    step = pl.program_id(0)
    columns = panel[...].reshape(-1, panel.shape[-1])
    left = jnp.concatenate([a[0], b[0]], axis=0)
    counts = jnp.concatenate([c0[...], c1[...]], axis=0)
    predicted = contract_last(left, columns)
    ratios = tile_ratios(counts, predicted, live_ref, step, tiles_across)
    total = jnp.dot(jnp.concatenate(ratios, axis=1), columns, preferred_element_type=F32)
    keep[0] = total[:BLOCK]
    send[0] = total[BLOCK:]


def columns_kernel(tiles_across, rows_ref, live_ref, c0, c1, a, b, panel, sums, rows_total):
    step = pl.program_id(0)

    @pl.when(step == 0)
    def _():
        sums[...] = jnp.zeros_like(sums)
        rows_total[...] = jnp.zeros_like(rows_total)

    columns = panel[...].reshape(-1, panel.shape[-1])
    left = jnp.concatenate([a[0], b[0]], axis=0)
    counts = jnp.concatenate([c0[...], c1[...]], axis=0)
    predicted = contract_last(left, columns)
    ratios = tile_ratios(counts, predicted, live_ref, step, tiles_across)
    rows_total[...] += jnp.sum(left.astype(F32).reshape(-1, 8, left.shape[-1]), axis=0)
    for j in range(tiles_across):
        term = lax.dot_general(
            ratios[j], left, (((0,), (0,)), ((), ())), preferred_element_type=F32
        )
        sums[2 * j] += term[:BLOCK]
        sums[2 * j + 1] += term[BLOCK:]


def sweep(kernel, rows_at, live, counts, own, other, panel, out_shape, out_specs):
    width = own.shape[-1]
    across = counts.shape[1]

    def counts_spec(half):
        return pl.BlockSpec((BLOCK, across), lambda g, rows, live: (rows[2 * g + half], 0))

    block = pl.BlockSpec((1, BLOCK, width), lambda g, rows, live: (g, 0, 0))
    grid_spec = pltpu.PrefetchScalarGridSpec(
        num_scalar_prefetch=2,
        grid=(8,),
        in_specs=[
            counts_spec(0),
            counts_spec(1),
            block,
            block,
            pl.BlockSpec(panel.shape, lambda g, rows, live: (0, 0, 0)),
        ],
        out_specs=out_specs,
    )
    flops = 4 * counts.shape[0] * across * width
    return pl.pallas_call(
        functools.partial(kernel, across // TILE),
        grid_spec=grid_spec,
        out_shape=out_shape,
        cost_estimate=pl.CostEstimate(
            flops=flops, bytes_accessed=4 * counts.size + 8 * own.size, transcendentals=0
        ),
        compiler_params=pltpu.CompilerParams(vmem_limit_bytes=48 * 2**20),
    )(rows_at, live, counts, counts, own, other, panel)


def exchange(blocks, axis):
    groups = CHIP_GROUPS if axis == "col" else None
    flat = blocks.reshape(-1, blocks.shape[-1])
    flat = lax.all_to_all(flat, axis, 0, 0, axis_index_groups=groups, tiled=True)
    return flat.reshape(blocks.shape)


def gather(block, axis):
    return exchange(jnp.broadcast_to(block[None], (8,) + block.shape), axis)


def split(value):
    high = lax.reduce_precision(value, exponent_bits=5, mantissa_bits=10)
    return [high.astype(WIRE), (value - high).astype(WIRE)]


def join(high, low):
    return high.astype(F32) + low.astype(F32)


def pack(blocks, extra):
    rows = jnp.stack(extra + [jnp.zeros_like(extra[0])] * (PAD - len(extra)))
    rows = jnp.broadcast_to(rows[None], (8,) + rows.shape)
    return jnp.concatenate([blocks.astype(WIRE), rows], axis=1)


def local(click_counts, tile_pattern, row_factors, column_factors):
    width = row_factors.shape[1]
    core = lax.axis_index("col") % 2
    steps = jnp.arange(8, dtype=jnp.int32)
    rows_at = jnp.stack([2 * steps + core, 2 * steps + 1 - core], axis=1).reshape(-1)
    live = tile_pattern.reshape(-1)

    with jax.named_scope("gather_in"):
        own = gather(row_factors, "col")
        other = lax.ppermute(own, "col", SWAP_CORE)
        panel = gather(column_factors, "row")
        column_total = jnp.sum(panel.astype(F32), axis=(0, 1))

    block = pl.BlockSpec((1, BLOCK, width), lambda g, rows, live: (g, 0, 0))
    keep, send = sweep(
        rows_kernel,
        rows_at,
        live,
        click_counts,
        own,
        other,
        panel,
        (
            jax.ShapeDtypeStruct((8, BLOCK, width), F32),
            jax.ShapeDtypeStruct((8, BLOCK, width), F32),
        ),
        (block, block),
    )
    with jax.named_scope("reduce_rows"):
        came = lax.ppermute(send, "col", SWAP_CORE)
        other_total = lax.ppermute(column_total, "col", SWAP_CORE)
        packed = pack((keep + came) * ROW_SCALE, split(column_total + other_total))
        came = exchange(packed, "col")
        share = jnp.sum(came[:, :BLOCK].astype(F32), axis=0) * (1 / ROW_SCALE)
        column_total = jnp.sum(join(came[:, BLOCK], came[:, BLOCK + 1]), axis=0)
        updated_rows = (row_factors.astype(F32) * share / column_total).astype(jnp.bfloat16)
    with jax.named_scope("gather_new"):
        own = gather(updated_rows, "col")
        other = lax.ppermute(own, "col", SWAP_CORE)
    sums, row_total = sweep(
        columns_kernel,
        rows_at,
        live,
        click_counts,
        own,
        other,
        panel,
        (
            jax.ShapeDtypeStruct((8, BLOCK, width), F32),
            jax.ShapeDtypeStruct((8, width), F32),
        ),
        (
            pl.BlockSpec((8, BLOCK, width), lambda g, rows, live: (0, 0, 0)),
            pl.BlockSpec((8, width), lambda g, rows, live: (0, 0)),
        ),
    )
    with jax.named_scope("reduce_columns"):
        row_total = jnp.sum(row_total, axis=0)
        fine = jnp.minimum(row_total * FINE_SCALE, FINE_LIMIT)
        packed = pack(sums * COLUMN_SCALE, split(row_total * COARSE_SCALE) + split(fine))
        came = exchange(packed, "row")
        share = jnp.sum(came[:, :BLOCK].astype(F32), axis=0) * (1 / COLUMN_SCALE)
        coarse = join(came[:, BLOCK], came[:, BLOCK + 1]) * (1 / COARSE_SCALE)
        fine = join(came[:, BLOCK + 2], came[:, BLOCK + 3])
        totals = jnp.where(fine < FINE_LIMIT, fine * (1 / FINE_SCALE), coarse)
        row_total = jnp.sum(totals, axis=0)
    updated_columns = (column_factors.astype(F32) * share / row_total).astype(jnp.bfloat16)
    return (updated_rows, updated_columns)


def solution(mesh):
    in_specs = (P("row", "col"), P("row", "col"), P(("row", "col"), None), P(("col", "row"), None))
    out_specs = (P(("row", "col"), None), P(("col", "row"), None))
    return jax.shard_map(local, mesh=mesh, in_specs=in_specs, out_specs=out_specs, check_vma=False)
```

```python
import functools

import jax
import jax.numpy as jnp
from jax import lax
from jax.experimental import pallas as pl
from jax.experimental.pallas import tpu as pltpu
from jax.sharding import PartitionSpec as P

WIRE = jnp.float16
ROW_SCALE = 2.0**-6
COLUMN_SCALE = 2.0**-9
COLUMN_STEPS = ((2.0**5, 1.0),)
ROW_STEPS = (
    (2.0**12, 2.0**-8),
    (2.0**4, 1.0),
    (2.0**-4, 2.0**8),
    (2.0**-12, 2.0**16),
    (2.0**-20, 2.0**24),
)
TINY = 1e-30
BLOCK = 128
TILE = 256
PAD = 8
F32 = jnp.float32
BF16 = jnp.bfloat16


def along_z(step):
    return [(j, (j // 4 + step) % 4 * 4 + j % 4) for j in range(16)]


def along_x(step):
    return [(i, (i // 2 + step) % 4 * 2 + i % 2) for i in range(8)]


def to_col(dz, dl):
    return [(j, (j // 4 + dz) % 4 * 4 + (j ^ (2 * dl)) % 4) for j in range(16)]


def to_row(dx, dh):
    return [(i, (i // 2 + dx) % 4 * 2 + (i ^ dh) % 2) for i in range(8)]


SWAP_CORE = [(j, j ^ 1) for j in range(16)]


AWAY = [(2, 1), (2, 0), (1, 1), (3, 1), (1, 0), (3, 0), (0, 1)]


def swap_core(value):
    return lax.ppermute(value, "col", SWAP_CORE)


def contract_last(a, b):
    return lax.dot_general(a, b, (((1,), (1,)), ((), ())), preferred_element_type=F32)


def contract_first(a, b):
    return lax.dot_general(a, b, (((0,), (0,)), ((), ())), preferred_element_type=F32)


def stage_kernel(tiles_across, rows_ref, live_ref, place_ref, counts, staged):
    step = pl.program_id(0)
    row_tile = rows_ref[step] // 2
    for k in range(2 * tiles_across):
        place = place_ref[k]
        start = pl.multiple_of(place * BLOCK, BLOCK)
        live = live_ref[row_tile * tiles_across + place // 2] > 0
        value = counts[:, pl.ds(start, BLOCK)].astype(F32)
        staged[0, :, k * BLOCK : (k + 1) * BLOCK] = jnp.where(live, value, 0.0)


def stage_counts(rows_at, live, columns_at, counts):
    across = counts.shape[1]
    grid_spec = pltpu.PrefetchScalarGridSpec(
        num_scalar_prefetch=3,
        grid=(16,),
        in_specs=[pl.BlockSpec((BLOCK, across), lambda g, rows, live, place: (rows[g], 0))],
        out_specs=pl.BlockSpec((1, BLOCK, across), lambda g, rows, live, place: (g, 0, 0)),
    )
    return pl.pallas_call(
        functools.partial(stage_kernel, across // TILE),
        grid_spec=grid_spec,
        out_shape=jax.ShapeDtypeStruct((16, BLOCK, across), F32),
        cost_estimate=pl.CostEstimate(
            flops=counts.size, bytes_accessed=8 * counts.size, transcendentals=0
        ),
        compiler_params=pltpu.CompilerParams(vmem_limit_bytes=8 * 2**20),
    )(rows_at, live, columns_at, counts)


def ratios_of(counts, left, columns):
    predicted = contract_last(left, columns)
    return (counts / jnp.maximum(predicted, TINY)).astype(BF16)


def total_rows(total, steps, last_scale):
    rows = []
    for unit, scale in steps:
        shift = 1.5 * 2.0**23 * unit
        part = (total + shift) - shift
        rows.append(part * scale)
        total = total - part
    rows.append(total * last_scale)
    rows += [jnp.zeros_like(total)] * (PAD - len(rows))
    return jnp.concatenate(rows, axis=0)


def join_total(rows, steps, last_scale, scale):
    scales = [s for _, s in steps] + [last_scale]
    return sum(rows[k].astype(F32) * (1 / (s * scale)) for k, s in enumerate(scales))


def rows_kernel(first, counts, a0, a1, b0, b1, panel, *refs):
    keep, send = refs[-2:]
    columns = panel[...].reshape(-1, panel.shape[-1])
    for e, (a, b) in enumerate(((a0, b0), (a1, b1))):
        left = jnp.concatenate([a[...], b[...]], axis=0)
        block = counts[first + 2 * e : first + 2 * e + 2].reshape(TILE, -1)
        total = jnp.dot(ratios_of(block, left, columns), columns, preferred_element_type=F32)
        keep[e, :BLOCK] = total[:BLOCK]
        send[e, :BLOCK] = total[BLOCK:]
    total = jnp.sum(columns.astype(F32), axis=0, keepdims=True)
    rows = total_rows(total, COLUMN_STEPS, 1.0)
    for e in range(2):
        keep[e, BLOCK:] = rows
        send[e, BLOCK:] = rows


def columns_kernel(at, first, last, counts, a0, a1, b0, b1, panel, *refs):
    if first:
        sums, rows_total = refs
    else:
        sums_in, total_in, sums, rows_total = refs
    columns = panel[...].reshape(-1, panel.shape[-1])
    left = jnp.concatenate([a0[...], b0[...], a1[...], b1[...]], axis=0)
    total = jnp.sum(left.astype(F32).reshape(-1, 8, left.shape[-1]), axis=0)
    if not first:
        total = total + total_in[...]
    rows_total[...] = total
    ratios = []
    for e in range(2):
        block = counts[at[e] : at[e] + 2].reshape(TILE, -1)
        ratios.append(ratios_of(block, left[e * TILE : (e + 1) * TILE], columns))
    ratios = jnp.concatenate(ratios, axis=0)
    for j in range(4):
        term = contract_first(ratios[:, j * TILE : (j + 1) * TILE], left)
        for k in range(2):
            part = term[k * BLOCK : (k + 1) * BLOCK]
            sums[2 * j + k, :BLOCK] = part if first else part + sums_in[2 * j + k, :BLOCK]
    if last:
        total = jnp.sum(total, axis=0, keepdims=True)
        rows = total_rows(total, ROW_STEPS, 2.0**24)
        for k in range(8):
            sums[k, BLOCK:] = rows * (1 / COLUMN_SCALE)


def call(kernel, operands, out_shape, aliases, after=()):
    vmem = pl.BlockSpec(memory_space=pltpu.VMEM)
    return pl.pallas_call(
        kernel,
        in_specs=[vmem] * len(operands) + [pl.BlockSpec(memory_space=pl.ANY)] * len(after),
        out_specs=(vmem,) * len(out_shape),
        out_shape=out_shape,
        input_output_aliases=aliases,
        cost_estimate=pl.CostEstimate(flops=2**20, bytes_accessed=2**16, transcendentals=0),
        compiler_params=pltpu.CompilerParams(vmem_limit_bytes=24 * 2**20),
    )(*operands, *after)


def after(value, other):
    return lax.optimization_barrier((value, other))[0]


def local(click_counts, tile_pattern, row_factors, column_factors):
    width = row_factors.shape[1]
    at_row, at_col = lax.axis_index("row"), lax.axis_index("col")
    z, pair, core = at_col // 4, at_col // 2 % 2, at_col % 2
    x, far = at_row // 2, at_row % 2
    rows_at = jnp.stack(
        [
            (z + dz) % 4 * 4 + (pair + dl) % 2 * 2 + (core + dc) % 2
            for dz in range(4)
            for dl in range(2)
            for dc in range(2)
        ]
    ).astype(jnp.int32)
    columns_at = jnp.stack(
        [(x + dx) % 4 * 2 + (far + dh) % 2 for dx in range(4) for dh in range(2)]
    ).astype(jnp.int32)
    live = tile_pattern.reshape(-1)

    counts = stage_counts(rows_at, live, columns_at, click_counts)
    with jax.named_scope("gather_in"):
        column_pair = jnp.stack([column_factors, lax.ppermute(column_factors, "row", to_row(0, 1))])
        row_pair = jnp.stack([row_factors, lax.ppermute(row_factors, "col", to_col(0, 1))])
        row_pair = after(row_pair, counts)
        own, panel = {0: row_pair}, {0: column_pair}
        for d in (2, 1, 3):
            panel[d] = lax.ppermute(column_pair, "row", along_x(-d))
            own[d] = lax.ppermute(row_pair, "col", along_z(-d))
        other = {d: swap_core(own[d]) for d in range(4)}
        panel = jnp.concatenate([panel[d] for d in range(4)])
    with jax.named_scope("reduce_rows"):
        piece = jax.ShapeDtypeStruct((2, BLOCK + PAD, width), F32)
        came, arrived, waits = {}, [], ()
        for d in (2, 1, 3, 0):
            a, b = own[d], other[d]
            keep, send = call(
                functools.partial(rows_kernel, 4 * d),
                (counts, a[0], a[1], b[0], b[1], panel),
                (piece, piece),
                {},
                waits,
            )
            came[d] = swap_core(send)
            partial = (keep + came[d]) * ROW_SCALE
            for e in (1, 0):
                if d or e:
                    arrived.append(lax.ppermute(partial[e].astype(WIRE), "col", to_col(d, e)))
            waits = {2: (keep,), 1: (came.get(2),), 3: (came.get(1),)}.get(d)
        partial = partial[0]
        for a in arrived:
            partial = partial + a.astype(F32)
        share = partial[:BLOCK] * (1 / ROW_SCALE)
        column_total = join_total(partial[BLOCK:], COLUMN_STEPS, 1.0, ROW_SCALE)
        updated_rows = (row_factors.astype(F32) * share / column_total).astype(BF16)
    with jax.named_scope("gather_new"):
        own = {(0, 0): updated_rows}
        for d, e in AWAY:
            own[d, e] = lax.ppermute(updated_rows, "col", to_col(-d, e))
        out_shape = (
            jax.ShapeDtypeStruct((8, BLOCK + PAD, width), F32),
            jax.ShapeDtypeStruct((8, width), F32),
        )
        steps = [((0, 0), AWAY[0]), AWAY[1:3], AWAY[3:5], AWAY[5:7]]
        other, history = {}, []
        for i, step in enumerate(steps):
            for k in step:
                ready = after(own[k], history[i - 2][0]) if i > 1 else own[k]
                other[k] = swap_core(ready)
            blocks = [own[k] for k in step] + [other[k] for k in step]
            sums = call(
                functools.partial(
                    columns_kernel, tuple(4 * d + 2 * e for d, e in step), i == 0, i == 3
                ),
                [counts] + blocks + [panel] + (list(history[-1]) if i else []),
                out_shape,
                {6: 0, 7: 1} if i else {},
            )
            history.append(sums)
        sums = sums[0]
    with jax.named_scope("reduce_columns"):
        partial = sums[0] * COLUMN_SCALE
        for d, e in AWAY:
            a = (sums[2 * d + e] * COLUMN_SCALE).astype(WIRE)
            partial = partial + lax.ppermute(a, "row", to_row(d, e)).astype(F32)
        share = partial[:BLOCK] * (1 / COLUMN_SCALE)
        row_total = join_total(partial[BLOCK:], ROW_STEPS, 2.0**24, 1.0)
        updated_columns = (column_factors.astype(F32) * share / row_total).astype(BF16)
    return (updated_rows, updated_columns)


def solution(mesh):
    in_specs = (P("row", "col"), P("row", "col"), P(("row", "col"), None), P(("col", "row"), None))
    out_specs = (P(("row", "col"), None), P(("col", "row"), None))
    return jax.shard_map(local, mesh=mesh, in_specs=in_specs, out_specs=out_specs, check_vma=False)
```

```python
import functools

import jax
import jax.numpy as jnp
from jax import lax
from jax.experimental import pallas as pl
from jax.experimental.pallas import tpu as pltpu
from jax.sharding import PartitionSpec as P

WIRE = jnp.float16
ROW_SCALE = 2.0**-6
COLUMN_SCALE = 2.0**-9
COLUMN_STEPS = ((2.0**5, 1.0),)
ROW_STEPS = (
    (2.0**12, 2.0**-8),
    (2.0**4, 1.0),
    (2.0**-4, 2.0**8),
    (2.0**-12, 2.0**16),
    (2.0**-20, 2.0**24),
)
TINY = 1e-30
BLOCK = 128
TILE = 256
PAD = 8
F32 = jnp.float32
BF16 = jnp.bfloat16


def along_z(step):
    return [(j, (j // 4 + step) % 4 * 4 + j % 4) for j in range(16)]


def along_x(step):
    return [(i, (i // 2 + step) % 4 * 2 + i % 2) for i in range(8)]


def to_col(dz, dl):
    return [(j, (j // 4 + dz) % 4 * 4 + (j ^ (2 * dl)) % 4) for j in range(16)]


def to_row(dx, dh):
    return [(i, (i // 2 + dx) % 4 * 2 + (i ^ dh) % 2) for i in range(8)]


SWAP_CORE = [(j, j ^ 1) for j in range(16)]


AWAY = [(2, 1), (2, 0), (1, 1), (3, 1), (1, 0), (3, 0), (0, 1)]


def swap_core(value):
    return lax.ppermute(value, "col", SWAP_CORE)


def contract_last(a, b):
    return lax.dot_general(a, b, (((1,), (1,)), ((), ())), preferred_element_type=F32)


def contract_first(a, b):
    return lax.dot_general(a, b, (((0,), (0,)), ((), ())), preferred_element_type=F32)


def stage_kernel(rows_ref, place_ref, live_ref, counts, staged, held, sems):
    copies = [
        pltpu.make_async_copy(
            counts.at[pl.ds(pl.multiple_of(rows_ref[g] * BLOCK, BLOCK), BLOCK)], held.at[g], sems.at[g]
        )
        for g in range(16)
    ]
    for copy in copies:
        copy.start()
    for g in range(16):
        copies[g].wait()
        for k in range(8):
            place = place_ref[k]
            start = pl.multiple_of(place * BLOCK, BLOCK)
            live = live_ref[place // 2, rows_ref[g] // 2] > 0
            value = held[g, :, pl.ds(start, BLOCK)].astype(F32)
            staged[g, :, k * BLOCK : (k + 1) * BLOCK] = jnp.where(live, value, 0.0)


def stage_counts(rows_at, columns_at, live, counts):
    across = counts.shape[1]
    smem = pl.BlockSpec(memory_space=pltpu.SMEM)
    return pl.pallas_call(
        stage_kernel,
        in_specs=[smem, smem, smem, pl.BlockSpec(memory_space=pltpu.HBM)],
        out_specs=pl.BlockSpec(memory_space=pltpu.VMEM),
        out_shape=jax.ShapeDtypeStruct((16, BLOCK, across), F32),
        scratch_shapes=[
            pltpu.VMEM((16, BLOCK, across), jnp.int32),
            pltpu.SemaphoreType.DMA((16,)),
        ],
        cost_estimate=pl.CostEstimate(
            flops=counts.size, bytes_accessed=8 * counts.size, transcendentals=0
        ),
        compiler_params=pltpu.CompilerParams(vmem_limit_bytes=44 * 2**20),
    )(rows_at, columns_at, live, counts)


def ratios_of(counts, left, columns):
    predicted = contract_last(left, columns)
    return (counts / jnp.maximum(predicted, TINY)).astype(BF16)


def total_rows(total, steps, last_scale):
    rows = []
    for unit, scale in steps:
        shift = 1.5 * 2.0**23 * unit
        part = (total + shift) - shift
        rows.append(part * scale)
        total = total - part
    rows.append(total * last_scale)
    rows += [jnp.zeros_like(total)] * (PAD - len(rows))
    return jnp.concatenate(rows, axis=0)


def join_total(rows, steps, last_scale, scale):
    scales = [s for _, s in steps] + [last_scale]
    return sum(rows[k].astype(F32) * (1 / (s * scale)) for k, s in enumerate(scales))


def rows_kernel(at, counts, panel, *refs):
    keep, send = refs[-2:]
    columns = panel[...].reshape(-1, panel.shape[-1])
    total = jnp.sum(columns.astype(F32), axis=0, keepdims=True)
    rows = total_rows(total, COLUMN_STEPS, 1.0)
    for e, first in enumerate(at):
        left = jnp.concatenate([refs[2 * e][...], refs[2 * e + 1][...]], axis=0)
        block = counts[first : first + 2].reshape(TILE, -1)
        total = jnp.dot(ratios_of(block, left, columns), columns, preferred_element_type=F32)
        keep[e, :BLOCK] = total[:BLOCK]
        send[e, :BLOCK] = total[BLOCK:]
        keep[e, BLOCK:] = rows
        send[e, BLOCK:] = rows


def columns_kernel(at, first, last, counts, a0, a1, b0, b1, panel, *refs):
    if first:
        sums, rows_total = refs
    else:
        sums_in, total_in, sums, rows_total = refs
    columns = panel[...].reshape(-1, panel.shape[-1])
    left = jnp.concatenate([a0[...], b0[...], a1[...], b1[...]], axis=0)
    total = jnp.sum(left.astype(F32).reshape(-1, 8, left.shape[-1]), axis=0)
    if not first:
        total = total + total_in[...]
    rows_total[...] = total
    ratios = []
    for e in range(2):
        block = counts[at[e] : at[e] + 2].reshape(TILE, -1)
        ratios.append(ratios_of(block, left[e * TILE : (e + 1) * TILE], columns))
    ratios = jnp.concatenate(ratios, axis=0)
    for j in range(4):
        term = contract_first(ratios[:, j * TILE : (j + 1) * TILE], left)
        for k in range(2):
            part = term[k * BLOCK : (k + 1) * BLOCK]
            sums[2 * j + k, :BLOCK] = part if first else part + sums_in[2 * j + k, :BLOCK]
    if last:
        total = jnp.sum(total, axis=0, keepdims=True)
        rows = total_rows(total, ROW_STEPS, 2.0**24)
        for k in range(8):
            sums[k, BLOCK:] = rows * (1 / COLUMN_SCALE)


def call(kernel, operands, out_shape, aliases, after=()):
    vmem = pl.BlockSpec(memory_space=pltpu.VMEM)
    return pl.pallas_call(
        kernel,
        in_specs=[vmem] * len(operands) + [pl.BlockSpec(memory_space=pl.ANY)] * len(after),
        out_specs=(vmem,) * len(out_shape),
        out_shape=out_shape,
        input_output_aliases=aliases,
        cost_estimate=pl.CostEstimate(flops=2**20, bytes_accessed=2**16, transcendentals=0),
        compiler_params=pltpu.CompilerParams(vmem_limit_bytes=24 * 2**20),
    )(*operands, *after)


def after(value, other):
    return lax.optimization_barrier((value, other))[0]


def local(click_counts, tile_pattern, row_factors, column_factors):
    width = row_factors.shape[1]
    at_row, at_col = lax.axis_index("row"), lax.axis_index("col")
    z, pair, core = at_col // 4, at_col // 2 % 2, at_col % 2
    x, far = at_row // 2, at_row % 2
    rows_at = jnp.stack(
        [
            (z + dz) % 4 * 4 + (pair + dl) % 2 * 2 + (core + dc) % 2
            for dz in range(4)
            for dl in range(2)
            for dc in range(2)
        ]
    ).astype(jnp.int32)
    columns_at = jnp.stack(
        [(x + dx) % 4 * 2 + (far + dh) % 2 for dx in range(4) for dh in range(2)]
    ).astype(jnp.int32)

    counts = stage_counts(rows_at, columns_at, tile_pattern.T, click_counts)
    with jax.named_scope("gather_in"):
        column_pair = jnp.stack([column_factors, lax.ppermute(column_factors, "row", to_row(0, 1))])
        row_pair = jnp.stack([row_factors, lax.ppermute(row_factors, "col", to_col(0, 1))])
        row_pair, column_pair, counts = lax.optimization_barrier((row_pair, column_pair, counts))
        own, panel = {0: row_pair}, {0: column_pair}
        for d in (2, 1, 3):
            panel[d] = lax.ppermute(column_pair, "row", along_x(-d))
            own[d] = lax.ppermute(row_pair, "col", along_z(-d))
        panel = jnp.concatenate([panel[d] for d in range(4)])
        other = {d: swap_core(own[d]) for d in range(4)}
    with jax.named_scope("reduce_rows"):
        came, arrived, waits = [], [], ()
        for step in ([(2, 1)], [(2, 0), (1, 1)], [(1, 0), (3, 1)], [(3, 0), (0, 1), (0, 0)]):
            piece = jax.ShapeDtypeStruct((len(step), BLOCK + PAD, width), F32)
            blocks = [b for d, e in step for b in (own[d][e], other[d][e])]
            keep, send = call(
                functools.partial(rows_kernel, tuple(4 * d + 2 * e for d, e in step)),
                [counts, panel] + blocks,
                (piece, piece),
                {},
                waits,
            )
            came.append(swap_core(send))
            partial = (keep + came[-1]) * ROW_SCALE
            for k, (d, e) in enumerate(step):
                if d or e:
                    arrived.append(lax.ppermute(partial[k].astype(WIRE), "col", to_col(d, e)))
            waits = (came[-2],) if len(came) > 1 else (keep,)
        partial = partial[2]
        for a in arrived:
            partial = partial + a.astype(F32)
        share = partial[:BLOCK] * (1 / ROW_SCALE)
        column_total = join_total(partial[BLOCK:], COLUMN_STEPS, 1.0, ROW_SCALE)
        updated_rows = (row_factors.astype(F32) * share / column_total).astype(BF16)
    with jax.named_scope("gather_new"):
        own = {(0, 0): updated_rows}
        for d, e in AWAY:
            own[d, e] = lax.ppermute(updated_rows, "col", to_col(-d, e))
        out_shape = (
            jax.ShapeDtypeStruct((8, BLOCK + PAD, width), F32),
            jax.ShapeDtypeStruct((8, width), F32),
        )
        steps = [((0, 0), AWAY[0]), AWAY[1:3], AWAY[3:5], AWAY[5:7]]
        other, history = {}, []
        for i, step in enumerate(steps):
            for k in step:
                ready = after(own[k], history[i - 2][0]) if i > 1 else own[k]
                other[k] = swap_core(ready)
            blocks = [own[k] for k in step] + [other[k] for k in step]
            sums = call(
                functools.partial(
                    columns_kernel, tuple(4 * d + 2 * e for d, e in step), i == 0, i == 3
                ),
                [counts] + blocks + [panel] + (list(history[-1]) if i else []),
                out_shape,
                {6: 0, 7: 1} if i else {},
            )
            history.append(sums)
        sums = sums[0]
    with jax.named_scope("reduce_columns"):
        partial = sums[0] * COLUMN_SCALE
        for d, e in AWAY:
            a = (sums[2 * d + e] * COLUMN_SCALE).astype(WIRE)
            partial = partial + lax.ppermute(a, "row", to_row(d, e)).astype(F32)
        share = partial[:BLOCK] * (1 / COLUMN_SCALE)
        row_total = join_total(partial[BLOCK:], ROW_STEPS, 2.0**24, 1.0)
        updated_columns = (column_factors.astype(F32) * share / row_total).astype(BF16)
    return (updated_rows, updated_columns)


def solution(mesh):
    in_specs = (P("row", "col"), P("row", "col"), P(("row", "col"), None), P(("col", "row"), None))
    out_specs = (P(("row", "col"), None), P(("col", "row"), None))
    return jax.shard_map(local, mesh=mesh, in_specs=in_specs, out_specs=out_specs, check_vma=False)
```

```python
import functools

import jax
import jax.numpy as jnp
from jax import lax
from jax.experimental import pallas as pl
from jax.experimental.pallas import tpu as pltpu
from jax.sharding import PartitionSpec as P

WIRE = jnp.float16
ROW_SCALE = 2.0**-6
COLUMN_SCALE = 2.0**-9
COLUMN_STEPS = ((2.0**5, 1.0),)
ROW_STEPS = (
    (2.0**12, 2.0**-8),
    (2.0**4, 1.0),
    (2.0**-4, 2.0**8),
    (2.0**-12, 2.0**16),
    (2.0**-20, 2.0**24),
)
TINY = 1e-30
BLOCK = 128
TILE = 256
PAD = 8
F32 = jnp.float32
BF16 = jnp.bfloat16


def along_z(step):
    return [(j, (j // 4 + step) % 4 * 4 + j % 4) for j in range(16)]


def along_x(step):
    return [(i, (i // 2 + step) % 4 * 2 + i % 2) for i in range(8)]


def to_col(dz, dl):
    return [(j, (j // 4 + dz) % 4 * 4 + (j ^ (2 * dl)) % 4) for j in range(16)]


def to_row(dx, dh):
    return [(i, (i // 2 + dx) % 4 * 2 + (i ^ dh) % 2) for i in range(8)]


SWAP_CORE = [(j, j ^ 1) for j in range(16)]


AWAY = [(0, 1), (1, 0), (3, 0), (1, 1), (3, 1), (2, 0), (2, 1)]


def swap_core(value):
    return lax.ppermute(value, "col", SWAP_CORE)


def contract_last(a, b):
    return lax.dot_general(a, b, (((1,), (1,)), ((), ())), preferred_element_type=F32)


def contract_first(a, b):
    return lax.dot_general(a, b, (((0,), (0,)), ((), ())), preferred_element_type=F32)


def stage_kernel(rows_ref, place_ref, live_ref, counts, staged, held, sems):
    copies = [
        pltpu.make_async_copy(
            counts.at[pl.ds(pl.multiple_of(rows_ref[g] * BLOCK, BLOCK), BLOCK)], held.at[g], sems.at[g]
        )
        for g in range(16)
    ]
    for copy in copies:
        copy.start()
    for g in range(16):
        copies[g].wait()
        for k in range(8):
            place = place_ref[k]
            start = pl.multiple_of(place * BLOCK, BLOCK)
            live = live_ref[place // 2, rows_ref[g] // 2] > 0
            value = held[g, :, pl.ds(start, BLOCK)].astype(F32)
            staged[g, :, k * BLOCK : (k + 1) * BLOCK] = jnp.where(live, value, 0.0)


def stage_counts(rows_at, columns_at, live, counts):
    across = counts.shape[1]
    smem = pl.BlockSpec(memory_space=pltpu.SMEM)
    return pl.pallas_call(
        stage_kernel,
        in_specs=[smem, smem, smem, pl.BlockSpec(memory_space=pltpu.HBM)],
        out_specs=pl.BlockSpec(memory_space=pltpu.VMEM),
        out_shape=jax.ShapeDtypeStruct((16, BLOCK, across), F32),
        scratch_shapes=[
            pltpu.VMEM((16, BLOCK, across), jnp.int32),
            pltpu.SemaphoreType.DMA((16,)),
        ],
        cost_estimate=pl.CostEstimate(
            flops=counts.size, bytes_accessed=8 * counts.size, transcendentals=0
        ),
        compiler_params=pltpu.CompilerParams(vmem_limit_bytes=44 * 2**20),
    )(rows_at, columns_at, live, counts)


def ratios_of(counts, left, columns):
    predicted = contract_last(left, columns)
    return (counts / jnp.maximum(predicted, TINY)).astype(BF16)


def total_rows(total, steps, last_scale):
    rows = []
    for unit, scale in steps:
        shift = 1.5 * 2.0**23 * unit
        part = (total + shift) - shift
        rows.append(part * scale)
        total = total - part
    rows.append(total * last_scale)
    rows += [jnp.zeros_like(total)] * (PAD - len(rows))
    return jnp.concatenate(rows, axis=0)


def join_total(rows, steps, last_scale, scale):
    scales = [s for _, s in steps] + [last_scale]
    return sum(rows[k].astype(F32) * (1 / (s * scale)) for k, s in enumerate(scales))


def rows_kernel(at, counts, panel, *refs):
    keep, send = refs[-2:]
    columns = panel[...].reshape(-1, panel.shape[-1])
    total = jnp.sum(columns.astype(F32), axis=0, keepdims=True)
    rows = total_rows(total, COLUMN_STEPS, 1.0)
    for e, first in enumerate(at):
        left = jnp.concatenate([refs[2 * e][...], refs[2 * e + 1][...]], axis=0)
        block = counts[first : first + 2].reshape(TILE, -1)
        total = jnp.dot(ratios_of(block, left, columns), columns, preferred_element_type=F32)
        keep[e, :BLOCK] = total[:BLOCK]
        send[e, :BLOCK] = total[BLOCK:]
        keep[e, BLOCK:] = rows
        send[e, BLOCK:] = rows


def columns_kernel(at, first, last, counts, a0, a1, b0, b1, panel, *refs):
    if first:
        sums, rows_total = refs
    else:
        sums_in, total_in, sums, rows_total = refs
    columns = panel[...].reshape(-1, panel.shape[-1])
    left = jnp.concatenate([a0[...], b0[...], a1[...], b1[...]], axis=0)
    total = jnp.sum(left.astype(F32).reshape(-1, 8, left.shape[-1]), axis=0)
    if not first:
        total = total + total_in[...]
    rows_total[...] = total
    ratios = []
    for e in range(2):
        block = counts[at[e] : at[e] + 2].reshape(TILE, -1)
        ratios.append(ratios_of(block, left[e * TILE : (e + 1) * TILE], columns))
    ratios = jnp.concatenate(ratios, axis=0)
    for j in range(4):
        term = contract_first(ratios[:, j * TILE : (j + 1) * TILE], left)
        for k in range(2):
            part = term[k * BLOCK : (k + 1) * BLOCK]
            sums[2 * j + k, :BLOCK] = part if first else part + sums_in[2 * j + k, :BLOCK]
    if last:
        total = jnp.sum(total, axis=0, keepdims=True)
        rows = total_rows(total, ROW_STEPS, 2.0**24)
        for k in range(8):
            sums[k, BLOCK:] = rows * (1 / COLUMN_SCALE)


def call(kernel, operands, out_shape, aliases, after=()):
    vmem = pl.BlockSpec(memory_space=pltpu.VMEM)
    return pl.pallas_call(
        kernel,
        in_specs=[vmem] * len(operands) + [pl.BlockSpec(memory_space=pl.ANY)] * len(after),
        out_specs=(vmem,) * len(out_shape),
        out_shape=out_shape,
        input_output_aliases=aliases,
        cost_estimate=pl.CostEstimate(flops=2**20, bytes_accessed=2**16, transcendentals=0),
        compiler_params=pltpu.CompilerParams(vmem_limit_bytes=24 * 2**20),
    )(*operands, *after)


def after(value, other):
    return lax.optimization_barrier((value, other))[0]


def local(click_counts, tile_pattern, row_factors, column_factors):
    width = row_factors.shape[1]
    at_row, at_col = lax.axis_index("row"), lax.axis_index("col")
    z, pair, core = at_col // 4, at_col // 2 % 2, at_col % 2
    x, far = at_row // 2, at_row % 2
    rows_at = jnp.stack(
        [
            (z + dz) % 4 * 4 + (pair + dl) % 2 * 2 + (core + dc) % 2
            for dz in range(4)
            for dl in range(2)
            for dc in range(2)
        ]
    ).astype(jnp.int32)
    columns_at = jnp.stack(
        [(x + dx) % 4 * 2 + (far + dh) % 2 for dx in range(4) for dh in range(2)]
    ).astype(jnp.int32)

    counts = stage_counts(rows_at, columns_at, tile_pattern.T, click_counts)
    with jax.named_scope("gather_in"):
        column_pair = jnp.stack([column_factors, lax.ppermute(column_factors, "row", to_row(0, 1))])
        row_pair = jnp.stack([row_factors, lax.ppermute(row_factors, "col", to_col(0, 1))])
        row_pair, column_pair, counts = lax.optimization_barrier((row_pair, column_pair, counts))
        own, panel = {0: row_pair}, {0: column_pair}
        for d in (2, 1, 3):
            panel[d] = lax.ppermute(column_pair, "row", along_x(-d))
            own[d] = lax.ppermute(row_pair, "col", along_z(-d))
        panel = jnp.concatenate([panel[d] for d in range(4)])
        other = {d: swap_core(own[d]) for d in range(4)}
    with jax.named_scope("reduce_rows"):
        came, arrived, waits = [], [], ()
        for step in ([(2, 1)], [(2, 0), (1, 1)], [(1, 0), (3, 1)], [(3, 0), (0, 1), (0, 0)]):
            piece = jax.ShapeDtypeStruct((len(step), BLOCK + PAD, width), F32)
            blocks = [b for d, e in step for b in (own[d][e], other[d][e])]
            keep, send = call(
                functools.partial(rows_kernel, tuple(4 * d + 2 * e for d, e in step)),
                [counts, panel] + blocks,
                (piece, piece),
                {},
                waits,
            )
            came.append(swap_core(send))
            partial = (keep + came[-1]) * ROW_SCALE
            for k, (d, e) in enumerate(step):
                if d or e:
                    arrived.append(lax.ppermute(partial[k].astype(WIRE), "col", to_col(d, e)))
            waits = (came[-2],) if len(came) > 1 else (keep,)
        partial = partial[2]
        for a in arrived:
            partial = partial + a.astype(F32)
        share = partial[:BLOCK] * (1 / ROW_SCALE)
        column_total = join_total(partial[BLOCK:], COLUMN_STEPS, 1.0, ROW_SCALE)
        updated_rows = (row_factors.astype(F32) * share / column_total).astype(BF16)
    with jax.named_scope("gather_new"):
        own = {(0, 0): updated_rows}
        for d, e in AWAY:
            own[d, e] = lax.ppermute(updated_rows, "col", to_col(-d, e))
        out_shape = (
            jax.ShapeDtypeStruct((8, BLOCK + PAD, width), F32),
            jax.ShapeDtypeStruct((8, width), F32),
        )
        steps = [((0, 0), AWAY[0]), AWAY[1:3], AWAY[3:5], AWAY[5:7]]
        other, history = {}, []
        for i, step in enumerate(steps):
            for k in step:
                ready = after(own[k], history[i - 2][0]) if i > 1 else own[k]
                other[k] = swap_core(ready)
            blocks = [own[k] for k in step] + [other[k] for k in step]
            sums = call(
                functools.partial(
                    columns_kernel, tuple(4 * d + 2 * e for d, e in step), i == 0, i == 3
                ),
                [counts] + blocks + [panel] + (list(history[-1]) if i else []),
                out_shape,
                {6: 0, 7: 1} if i else {},
            )
            history.append(sums)
        sums = sums[0]
    with jax.named_scope("reduce_columns"):
        partial = sums[0] * COLUMN_SCALE
        for d, e in ((0, 1), (1, 0), (3, 0), (2, 1), (1, 1), (3, 1), (2, 0)):
            a = (sums[2 * d + e] * COLUMN_SCALE).astype(WIRE)
            partial = partial + lax.ppermute(a, "row", to_row(d, e)).astype(F32)
        share = partial[:BLOCK] * (1 / COLUMN_SCALE)
        row_total = join_total(partial[BLOCK:], ROW_STEPS, 2.0**24, 1.0)
        updated_columns = (column_factors.astype(F32) * share / row_total).astype(BF16)
    return (updated_rows, updated_columns)


def solution(mesh):
    in_specs = (P("row", "col"), P("row", "col"), P(("row", "col"), None), P(("col", "row"), None))
    out_specs = (P(("row", "col"), None), P(("col", "row"), None))
    return jax.shard_map(local, mesh=mesh, in_specs=in_specs, out_specs=out_specs, check_vma=False)
```

```python
import functools

import jax
import jax.numpy as jnp
from jax import lax
from jax.experimental import pallas as pl
from jax.experimental.pallas import tpu as pltpu
from jax.sharding import PartitionSpec as P

WIRE = jnp.float16
ROW_SCALE = 2.0**-6
COLUMN_SCALE = 2.0**-9
COLUMN_STEPS = ((2.0**5, 1.0),)
ROW_STEPS = (
    (2.0**12, 2.0**-8),
    (2.0**4, 1.0),
    (2.0**-4, 2.0**8),
    (2.0**-12, 2.0**16),
    (2.0**-20, 2.0**24),
)
TINY = 1e-30
BLOCK = 128
TILE = 256
PAD = 8
F32 = jnp.float32
BF16 = jnp.bfloat16


def along_z(step):
    return [(j, (j // 4 + step) % 4 * 4 + j % 4) for j in range(16)]


def along_x(step):
    return [(i, (i // 2 + step) % 4 * 2 + i % 2) for i in range(8)]


def to_col(dz, dl):
    return [(j, (j // 4 + dz) % 4 * 4 + (j ^ (2 * dl)) % 4) for j in range(16)]


def to_row(dx, dh):
    return [(i, (i // 2 + dx) % 4 * 2 + (i ^ dh) % 2) for i in range(8)]


SWAP_CORE = [(j, j ^ 1) for j in range(16)]


AWAY = [(0, 1), (1, 0), (3, 0), (1, 1), (3, 1), (2, 0), (2, 1)]


def swap_core(value):
    return lax.ppermute(value, "col", SWAP_CORE)


def contract_last(a, b):
    return lax.dot_general(a, b, (((1,), (1,)), ((), ())), preferred_element_type=F32)


def contract_first(a, b):
    return lax.dot_general(a, b, (((0,), (0,)), ((), ())), preferred_element_type=F32)


def stage_kernel(rows_ref, place_ref, live_ref, counts, staged, held, sems):
    copies = [
        pltpu.make_async_copy(
            counts.at[pl.ds(pl.multiple_of(rows_ref[g] * BLOCK, BLOCK), BLOCK)], held.at[g], sems.at[g]
        )
        for g in range(16)
    ]
    for copy in copies:
        copy.start()
    for g in range(16):
        copies[g].wait()
        for k in range(8):
            place = place_ref[k]
            start = pl.multiple_of(place * BLOCK, BLOCK)
            live = live_ref[place // 2, rows_ref[g] // 2] > 0
            value = held[g, :, pl.ds(start, BLOCK)].astype(F32)
            staged[g, :, k * BLOCK : (k + 1) * BLOCK] = jnp.where(live, value, 0.0)


def stage_counts(rows_at, columns_at, live, counts):
    across = counts.shape[1]
    smem = pl.BlockSpec(memory_space=pltpu.SMEM)
    return pl.pallas_call(
        stage_kernel,
        in_specs=[smem, smem, smem, pl.BlockSpec(memory_space=pltpu.HBM)],
        out_specs=pl.BlockSpec(memory_space=pltpu.VMEM),
        out_shape=jax.ShapeDtypeStruct((16, BLOCK, across), F32),
        scratch_shapes=[
            pltpu.VMEM((16, BLOCK, across), jnp.int32),
            pltpu.SemaphoreType.DMA((16,)),
        ],
        cost_estimate=pl.CostEstimate(
            flops=counts.size, bytes_accessed=8 * counts.size, transcendentals=0
        ),
        compiler_params=pltpu.CompilerParams(vmem_limit_bytes=44 * 2**20),
    )(rows_at, columns_at, live, counts)


def ratios_of(counts, left, columns):
    predicted = contract_last(left, columns)
    return (counts / jnp.maximum(predicted, TINY)).astype(BF16)


def total_rows(total, steps, last_scale):
    rows = []
    for unit, scale in steps:
        shift = 1.5 * 2.0**23 * unit
        part = (total + shift) - shift
        rows.append(part * scale)
        total = total - part
    rows.append(total * last_scale)
    rows += [jnp.zeros_like(total)] * (PAD - len(rows))
    return jnp.concatenate(rows, axis=0)


def join_total(rows, steps, last_scale, scale):
    scales = [s for _, s in steps] + [last_scale]
    return sum(rows[k].astype(F32) * (1 / (s * scale)) for k, s in enumerate(scales))


def rows_kernel(at, counts, panel, *refs):
    keep, send = refs[-2:]
    columns = panel[...].reshape(-1, panel.shape[-1])
    total = jnp.sum(columns.astype(F32), axis=0, keepdims=True)
    rows = total_rows(total, COLUMN_STEPS, 1.0)
    for e, first in enumerate(at):
        left = jnp.concatenate([refs[2 * e][...], refs[2 * e + 1][...]], axis=0)
        block = counts[first : first + 2].reshape(TILE, -1)
        total = jnp.dot(ratios_of(block, left, columns), columns, preferred_element_type=F32)
        keep[e, :BLOCK] = total[:BLOCK]
        send[e, :BLOCK] = total[BLOCK:]
        keep[e, BLOCK:] = rows
        send[e, BLOCK:] = rows


def columns_kernel(at, first, last, counts, a0, a1, b0, b1, panel, *refs):
    if first:
        sums, rows_total = refs
    else:
        sums_in, total_in, sums, rows_total = refs
    columns = panel[...].reshape(-1, panel.shape[-1])
    left = jnp.concatenate([a0[...], b0[...], a1[...], b1[...]], axis=0)
    total = jnp.sum(left.astype(F32).reshape(-1, 8, left.shape[-1]), axis=0)
    if not first:
        total = total + total_in[...]
    rows_total[...] = total
    ratios = []
    for e in range(2):
        block = counts[at[e] : at[e] + 2].reshape(TILE, -1)
        ratios.append(ratios_of(block, left[e * TILE : (e + 1) * TILE], columns))
    ratios = jnp.concatenate(ratios, axis=0)
    for j in range(4):
        term = contract_first(ratios[:, j * TILE : (j + 1) * TILE], left)
        for k in range(2):
            part = term[k * BLOCK : (k + 1) * BLOCK]
            sums[2 * j + k, :BLOCK] = part if first else part + sums_in[2 * j + k, :BLOCK]
    if last:
        total = jnp.sum(total, axis=0, keepdims=True)
        rows = total_rows(total, ROW_STEPS, 2.0**24)
        for k in range(8):
            sums[k, BLOCK:] = rows * (1 / COLUMN_SCALE)


def call(kernel, operands, out_shape, aliases, after=()):
    vmem = pl.BlockSpec(memory_space=pltpu.VMEM)
    return pl.pallas_call(
        kernel,
        in_specs=[vmem] * len(operands) + [pl.BlockSpec(memory_space=pl.ANY)] * len(after),
        out_specs=(vmem,) * len(out_shape),
        out_shape=out_shape,
        input_output_aliases=aliases,
        cost_estimate=pl.CostEstimate(flops=2**30, bytes_accessed=2**24, transcendentals=0),
        compiler_params=pltpu.CompilerParams(vmem_limit_bytes=24 * 2**20),
    )(*operands, *after)


def after(value, other):
    return lax.optimization_barrier((value, other))[0]


def local(click_counts, tile_pattern, row_factors, column_factors):
    width = row_factors.shape[1]
    at_row, at_col = lax.axis_index("row"), lax.axis_index("col")
    z, pair, core = at_col // 4, at_col // 2 % 2, at_col % 2
    x, far = at_row // 2, at_row % 2
    rows_at = jnp.stack(
        [
            (z + dz) % 4 * 4 + (pair + dl) % 2 * 2 + (core + dc) % 2
            for dz in range(4)
            for dl in range(2)
            for dc in range(2)
        ]
    ).astype(jnp.int32)
    columns_at = jnp.stack(
        [(x + dx) % 4 * 2 + (far + dh) % 2 for dx in range(4) for dh in range(2)]
    ).astype(jnp.int32)

    counts = stage_counts(rows_at, columns_at, tile_pattern.T, click_counts)
    with jax.named_scope("gather_in"):
        column_pair = jnp.stack([column_factors, lax.ppermute(column_factors, "row", to_row(0, 1))])
        row_pair = jnp.stack([row_factors, lax.ppermute(row_factors, "col", to_col(0, 1))])
        row_pair, column_pair, counts = lax.optimization_barrier((row_pair, column_pair, counts))
        own, panel = {0: row_pair}, {0: column_pair}
        for d in (1, 3, 2):
            panel[d] = lax.ppermute(column_pair, "row", along_x(-d))
            own[d] = lax.ppermute(row_pair, "col", along_z(-d))
        panel = jnp.concatenate([panel[d] for d in range(4)])
        other = {d: swap_core(own[d]) for d in range(4)}
    with jax.named_scope("reduce_rows"):
        came, arrived, waits = [], [], ()
        for step in ([(2, 1)], [(2, 0), (1, 1)], [(1, 0), (3, 1)], [(3, 0), (0, 1), (0, 0)]):
            piece = jax.ShapeDtypeStruct((len(step), BLOCK + PAD, width), F32)
            blocks = [b for d, e in step for b in (own[d][e], other[d][e])]
            keep, send = call(
                functools.partial(rows_kernel, tuple(4 * d + 2 * e for d, e in step)),
                [counts, panel] + blocks,
                (piece, piece),
                {},
                waits,
            )
            came.append(swap_core(send))
            partial = (keep + came[-1]) * ROW_SCALE
            for k, (d, e) in enumerate(step):
                if d or e:
                    arrived.append(lax.ppermute(partial[k].astype(WIRE), "col", to_col(d, e)))
            waits = (came[-2],) if len(came) > 1 else (keep,)
        partial = partial[2]
        for a in arrived:
            partial = partial + a.astype(F32)
        share = partial[:BLOCK] * (1 / ROW_SCALE)
        column_total = join_total(partial[BLOCK:], COLUMN_STEPS, 1.0, ROW_SCALE)
        updated_rows = (row_factors.astype(F32) * share / column_total).astype(BF16)
    with jax.named_scope("gather_new"):
        own = {(0, 0): updated_rows}
        for d, e in AWAY:
            own[d, e] = lax.ppermute(updated_rows, "col", to_col(-d, e))
        out_shape = (
            jax.ShapeDtypeStruct((8, BLOCK + PAD, width), F32),
            jax.ShapeDtypeStruct((8, width), F32),
        )
        steps = [((0, 0), AWAY[0]), AWAY[1:3], AWAY[3:5], AWAY[5:7]]
        other, history = {}, []
        for i, step in enumerate(steps):
            for k in step:
                ready = after(own[k], history[i - 2][0]) if i > 1 else own[k]
                other[k] = swap_core(ready)
            blocks = [own[k] for k in step] + [other[k] for k in step]
            sums = call(
                functools.partial(
                    columns_kernel, tuple(4 * d + 2 * e for d, e in step), i == 0, i == 3
                ),
                [counts] + blocks + [panel] + (list(history[-1]) if i else []),
                out_shape,
                {6: 0, 7: 1} if i else {},
            )
            history.append(sums)
        sums = sums[0]
    with jax.named_scope("reduce_columns"):
        partial = sums[0] * COLUMN_SCALE
        for d, e in ((0, 1), (1, 0), (3, 0), (2, 1), (1, 1), (3, 1), (2, 0)):
            a = (sums[2 * d + e] * COLUMN_SCALE).astype(WIRE)
            partial = partial + lax.ppermute(a, "row", to_row(d, e)).astype(F32)
        share = partial[:BLOCK] * (1 / COLUMN_SCALE)
        row_total = join_total(partial[BLOCK:], ROW_STEPS, 2.0**24, 1.0)
        updated_columns = (column_factors.astype(F32) * share / row_total).astype(BF16)
    return (updated_rows, updated_columns)


def solution(mesh):
    in_specs = (P("row", "col"), P("row", "col"), P(("row", "col"), None), P(("col", "row"), None))
    out_specs = (P(("row", "col"), None), P(("col", "row"), None))
    return jax.shard_map(local, mesh=mesh, in_specs=in_specs, out_specs=out_specs, check_vma=False)
```
